256 devices in a mesh: dp: 8 (over z_lo, x), seq: 32 (over z_hi, y, core).
Axes of the slice: x: 4, y: 4, z: 8 (z_hi: 4, z_lo: 2; z = z_hi * 2 + z_lo), core: 2. Of those that a mesh axis runs over, the one named last changes fastest.
Arguments:
- inputs: bfloat16 [128, 1024, 1024], P('seq', 'dp'), may hold values from -6 to 6
- gates: bfloat16 [128, 1024, 1024], P('seq', 'dp'), may hold values from -6 to 6
- kernel: bfloat16 [128, 1024, 1024], P('seq', 'dp'), may hold values from -5 to 5
- first_factor: bfloat16 [1024, 1024], replicated, may hold values from -0.1875 to 0.1875
- second_factor: bfloat16 [128, 128], replicated, may hold values from -0.5 to 0.5
- upstream: bfloat16 [128, 1024, 1024], P('seq', 'dp'), may hold values from -6 to 6
Outputs:
- output: bfloat16 [128, 1024, 1024], P('seq', 'dp')
- grad_inputs: bfloat16 [128, 1024, 1024], P('seq', 'dp')
- grad_gates: bfloat16 [128, 1024, 1024], P('seq', 'dp')
- grad_kernel: bfloat16 [128, 1024, 1024], P('seq', 'dp')
- grad_first: float32 [1024, 1024], P('seq')
- grad_second: float32 [128, 128], P('seq')
The draws below stay inside these ranges and needn't reach their ends.
All inputs are finite; a program needn't handle non-finite values.
Results may differ from the reference program's by a relative error of at most 0.0065.
Values may be sent and summed in bfloat16 or wider, within the bound.
No kernel may reach another device: no remote copies, remote signals or barrier semaphores. Data moves between devices by JAX's collectives and lax.ppermute only.
A program may use at most 64 MiB of HBM per device.

```python
import math
import jax
import jax.numpy as jnp

BS = 1024
NB = 128
C = 1024


def block_scale(rng, extent, split, smallest, largest):
    level, own = 1.0, jax.random.fold_in(rng, 6)
    for axis_at, parts in split:
        heights = jnp.exp(jax.random.uniform(jax.random.fold_in(own, axis_at), (parts,), jnp.float32, smallest / len(split), largest / len(split)))
        level = level * jnp.repeat(heights, extent[axis_at] // parts).reshape([-1 if axis == axis_at else 1 for axis in range(len(extent))])
    return level


def bell_draw(rng, shape, scale, limit, split=(), kind=jnp.bfloat16):
    factor_of = block_scale(rng, shape, split, -0.22, 0.18) if split else 1.0
    values = jax.random.normal(rng, shape, jnp.float32) * scale * factor_of
    return jnp.minimum(jnp.maximum(values, -limit), limit).astype(kind)


def setup_inputs(seed: int = 0) -> dict:
    splits = jax.random.split(jax.random.key(seed), 7)
    inputs = bell_draw(splits[0], (NB, C, BS), 1.0, 6.0, ((0, 32), (1, 8)))
    gates = bell_draw(splits[1], (NB, C, BS), 1.5, 6.0, ((0, 32), (1, 8)))
    kernel = bell_draw(splits[2], (NB, C, BS), 1.0, 5.0, ((0, 32), (1, 8)))
    first_factor = bell_draw(splits[3], (BS, BS), BS ** -0.5, 0.1875)
    second_factor = bell_draw(splits[4], (NB, NB), NB ** -0.5, 0.5)
    upstream = bell_draw(splits[5], (NB, C, BS), 1.0, 6.0, ((0, 32), (1, 8)))
    return dict(inputs=inputs, gates=gates, kernel=kernel, first_factor=first_factor, second_factor=second_factor, upstream=upstream)


def reference(inputs, gates, kernel, first_factor, second_factor, upstream):
    sig = jax.nn.sigmoid(gates.astype(jnp.float32))
    mixed_in = (inputs.astype(jnp.float32) * sig).astype(jnp.bfloat16)
    flat_in = mixed_in.reshape(NB * C, BS)
    blocks = jnp.dot(flat_in, first_factor.T, preferred_element_type=jnp.float32).astype(jnp.bfloat16).reshape(NB, C, BS)
    kerneled = (blocks.astype(jnp.float32) * kernel.astype(jnp.float32)).astype(jnp.bfloat16)
    flat_kern = kerneled.reshape(NB, C * BS)
    output = jnp.dot(second_factor, flat_kern, preferred_element_type=jnp.float32).astype(jnp.bfloat16).reshape(NB, C, BS)
    flat_up = upstream.reshape(NB, C * BS)
    grad_mid = jnp.dot(second_factor.T, flat_up, preferred_element_type=jnp.float32).astype(jnp.bfloat16).reshape(NB, C, BS)
    grad_kernel = (grad_mid.astype(jnp.float32) * blocks.astype(jnp.float32)).astype(jnp.bfloat16)
    grad_blocks = (grad_mid.astype(jnp.float32) * kernel.astype(jnp.float32)).astype(jnp.bfloat16)
    flat_grad = grad_blocks.reshape(NB * C, BS)
    grad_mixed = jnp.dot(flat_grad, first_factor, preferred_element_type=jnp.float32).reshape(NB, C, BS)
    grad_inputs = (grad_mixed * sig).astype(jnp.bfloat16)
    grad_gates = (grad_mixed * inputs.astype(jnp.float32) * sig * (1.0 - sig)).astype(jnp.bfloat16)
    grad_first = jnp.dot(flat_grad.T, flat_in, preferred_element_type=jnp.float32) / math.sqrt(NB * C)
    grad_second = jnp.dot(flat_up, flat_kern.T, preferred_element_type=jnp.float32) / math.sqrt(C * BS)
    return (output, grad_inputs, grad_gates, grad_kernel, grad_first, grad_second)
```

```python
import functools
import math

import jax
import jax.numpy as jnp
from jax import lax
from jax.experimental import pallas as pl
from jax.experimental.pallas import tpu as pltpu
from jax.sharding import Mesh
from jax.sharding import PartitionSpec as P

AXES = ("zl", "x", "zh", "y", "c")
BF = jnp.bfloat16
F32 = jnp.float32
PEERS, LOCAL, ROWS, HALF = 16, 4, 8, 512
CHANNELS, WIDTH = PEERS * ROWS, 2 * HALF
NB = PEERS * 2 * LOCAL
SIDE = PEERS * LOCAL * ROWS
LIMIT = 32 * 1024 * 1024


def swap(value):
    return lax.ppermute(value, "c", [(0, 1), (1, 0)])


def flip(value, axis, bit):
    size = lax.axis_size(axis)
    return lax.ppermute(value, axis, [(i, i ^ bit) for i in range(size)])


def shift(value, axis, step):
    size = lax.axis_size(axis)
    return lax.ppermute(value, axis, [(i, (i + step) % size) for i in range(size)])


def exchange(value):
    return lax.all_to_all(value, ("zh", "y"), 0, 0, tiled=True)


def after(value, *others):
    return lax.optimization_barrier((value,) + others)[0]


def to_owner():
    perm = []
    for zl in range(2):
        for x in range(4):
            for zh in range(4):
                for y in range(4):
                    for c in range(2):
                        place = 16 * c + 4 * x + y
                        source = (((zl * 4 + x) * 4 + zh) * 4 + y) * 2 + c
                        target = (((zl * 4 + zh) * 4 + place // 8) * 4 + place // 2 % 4) * 2 + place % 2
                        perm.append((source, target))
    return perm


def call(body, scalars, operands, in_specs, out_shapes, out_specs, grid=(1,), scratch=(), flops=0, moved=0):
    return pl.pallas_call(
        body,
        out_shape=out_shapes,
        grid_spec=pltpu.PrefetchScalarGridSpec(
            num_scalar_prefetch=len(scalars),
            grid=grid,
            in_specs=in_specs,
            out_specs=out_specs,
            scratch_shapes=list(scratch),
        ),
        compiler_params=pltpu.CompilerParams(vmem_limit_bytes=LIMIT),
        cost_estimate=pl.CostEstimate(flops=flops, bytes_accessed=moved, transcendentals=0),
    )(*scalars, *operands)


def whole(shape):
    return pl.BlockSpec(shape, lambda *_: (0,) * len(shape))


def struct(shape, dtype=BF):
    return jax.ShapeDtypeStruct(shape, dtype)


def sigmoid(gates):
    return jax.nn.sigmoid(gates.astype(F32))


def pack_body(in_ref, out_ref):
    for b in range(LOCAL):
        out_ref[:, b] = in_ref[b].reshape(PEERS, ROWS, WIDTH)


def pack(value):
    return call(
        pack_body,
        (),
        (value,),
        [whole((LOCAL, CHANNELS, WIDTH))],
        struct((PEERS, LOCAL, ROWS, WIDTH)),
        whole((PEERS, LOCAL, ROWS, WIDTH)),
        moved=4 << 20,
    )


def widen_body(core_ref, sf_ref, wide_ref, turned_ref):
    core = core_ref[0]
    size = 2 * SIDE
    n = lax.broadcasted_iota(jnp.int32, (size, NB), 0)
    o = lax.broadcasted_iota(jnp.int32, (size, NB), 1)
    rel = n // SIDE
    real = rel + core - 2 * rel * core
    source = (n // (LOCAL * ROWS)) % PEERS * (2 * LOCAL) + real * LOCAL + (n // ROWS) % LOCAL
    pick = jnp.where(source == o, 1.0, 0.0).astype(BF)
    row = lax.broadcasted_iota(jnp.int32, (size, size), 0) % ROWS
    column = lax.broadcasted_iota(jnp.int32, (size, size), 1) % ROWS
    same = row == column
    for ref, dim in ((wide_ref, 0), (turned_ref, 1)):
        tall = lax.dot_general(pick, sf_ref[...], (((1,), (dim,)), ((), ())), preferred_element_type=F32)
        full = lax.dot_general(tall.astype(BF), pick, (((1,), (1,)), ((), ())), preferred_element_type=F32)
        ref[...] = jnp.where(same, full, 0.0).astype(BF)


def widen(core, sf):
    shape = (2 * SIDE, 2 * SIDE)
    return call(
        widen_body,
        (core,),
        (sf,),
        [whole((NB, NB))],
        [struct(shape), struct(shape)],
        [whole(shape), whole(shape)],
        flops=1 << 30,
        moved=4 << 20,
    )


GROUP = 4
STEP_ROWS = GROUP * LOCAL * ROWS


def forward_body(
    core_ref, in_ref, gate_ref, kernel_ref, ff_ref, mixed_ref, blocks_ref, own_ref, oth_ref, kown_ref, koth_ref, flat
):
    core = core_ref[0]
    for b in range(LOCAL):
        mixed = (in_ref[b].astype(F32) * sigmoid(gate_ref[b])).astype(BF)
        for g in range(GROUP):
            piece = mixed[g * ROWS : (g + 1) * ROWS]
            mixed_ref[g, b] = piece
            flat[(g * LOCAL + b) * ROWS : (g * LOCAL + b + 1) * ROWS] = piece
    blocks = lax.dot_general(flat[...], ff_ref[...], (((1,), (1,)), ((), ())), preferred_element_type=F32)
    blocks = blocks.astype(BF).reshape(GROUP, LOCAL, ROWS, WIDTH)
    blocks_ref[...] = blocks
    for b in range(LOCAL):
        weight = kernel_ref[b].reshape(GROUP, ROWS, WIDTH)
        kern = (blocks[:, b].astype(F32) * weight.astype(F32)).astype(BF)
        low, high = kern[..., :HALF], kern[..., HALF:]
        own_ref[:, b] = jnp.where(core == 0, low, high)
        oth_ref[:, b] = jnp.where(core == 0, high, low)
        low, high = weight[..., :HALF], weight[..., HALF:]
        kown_ref[:, b] = jnp.where(core == 0, low, high)
        koth_ref[:, b] = jnp.where(core == 0, high, low)


def natural_spec():
    return pl.BlockSpec((LOCAL, GROUP * ROWS, WIDTH), lambda i, *_: (0, i, 0))


def rows_spec(width):
    return pl.BlockSpec((GROUP, LOCAL, ROWS, width), lambda i, *_: (i, 0, 0, 0))


def forward(core, inputs, gates, kernel, ff):
    full, part = struct((PEERS, LOCAL, ROWS, WIDTH)), struct((PEERS, LOCAL, ROWS, HALF))
    return call(
        forward_body,
        (core,),
        (inputs, gates, kernel, ff),
        [natural_spec()] * 3 + [whole((WIDTH, WIDTH))],
        [full, full, part, part, part, part],
        [rows_spec(WIDTH)] * 2 + [rows_spec(HALF)] * 4,
        grid=(PEERS // GROUP,),
        scratch=[pltpu.VMEM((STEP_ROWS, WIDTH), BF)],
        flops=1 << 30,
        moved=9 << 20,
    )


CHUNK = 256


def across_body(core_ref, wide_ref, own_ref, oth_ref, out_ref):
    own = own_ref[...].reshape(SIDE, CHUNK)
    oth = oth_ref[...].reshape(SIDE, CHUNK)
    total = jnp.dot(wide_ref[:, :SIDE], own, preferred_element_type=F32)
    total = total + jnp.dot(wide_ref[:, SIDE:], oth, preferred_element_type=F32)
    total = total.astype(BF)
    for rel in range(2):
        out_ref[:, rel] = total[rel * SIDE : (rel + 1) * SIDE].reshape(PEERS, LOCAL, ROWS, CHUNK)


def across(core, wide, own, oth):
    steps = HALF // CHUNK
    block = (PEERS, LOCAL, ROWS, CHUNK)
    if own.shape[-1] == WIDTH:
        own_spec = pl.BlockSpec(block, lambda i, core: (0, 0, 0, core[0] * steps + i))
    else:
        own_spec = pl.BlockSpec(block, lambda i, core: (0, 0, 0, i))
    return call(
        across_body,
        (core,),
        (wide, own, oth),
        [whole((2 * SIDE, 2 * SIDE)), own_spec, pl.BlockSpec(block, lambda i, core: (0, 0, 0, i))],
        struct((PEERS, 2, LOCAL, ROWS, HALF)),
        pl.BlockSpec((PEERS, 2, LOCAL, ROWS, CHUNK), lambda i, core: (0, 0, 0, 0, i)),
        grid=(steps,),
        flops=1 << 30,
        moved=4 << 20,
    )


def second_body(core_ref, up_ref, up_oth_ref, own_ref, oth_ref, out_ref):
    core = core_ref[0]
    size = 2 * SIDE
    ups = [ref[...].reshape(SIDE, HALF) for ref in (up_ref, up_oth_ref)]
    kerns = [ref[...].reshape(SIDE, HALF) for ref in (own_ref, oth_ref)]
    row = lax.broadcasted_iota(jnp.int32, (SIDE, SIDE), 0) % ROWS
    column = lax.broadcasted_iota(jnp.int32, (SIDE, SIDE), 1) % ROWS
    same = row == column
    n = lax.broadcasted_iota(jnp.int32, (size, NB), 0)
    o = lax.broadcasted_iota(jnp.int32, (size, NB), 1)

    def place(m, per):
        rel = m // (PEERS * LOCAL * per)
        real = rel + core - 2 * rel * core
        return (m // (LOCAL * per)) % PEERS * (2 * LOCAL) + real * LOCAL + (m // per) % LOCAL

    pick = jnp.where(place(n, ROWS) == o, 1.0, 0.0)
    tall = []
    for up in ups:
        wide = []
        for kern in kerns:
            full = lax.dot_general(up, kern, (((1,), (1,)), ((), ())), preferred_element_type=F32)
            full = jnp.where(same, full, 0.0).reshape(SIDE // ROWS, ROWS, SIDE)
            wide.append(full.sum(1))
        tall.append(jnp.concatenate(wide, 1))
    tall = jnp.concatenate(tall, 0)
    total = jnp.dot(tall, pick, precision=lax.Precision.HIGHEST, preferred_element_type=F32)
    n = lax.broadcasted_iota(jnp.int32, (NB, NB), 1)
    o = lax.broadcasted_iota(jnp.int32, (NB, NB), 0)
    pick = jnp.where(place(n, 1) == o, 1.0, 0.0)
    out_ref[...] = jnp.dot(pick, total, precision=lax.Precision.HIGHEST, preferred_element_type=F32)


def second(core, up, up_oth, own, oth):
    block = (PEERS, LOCAL, ROWS, HALF)
    return call(
        second_body,
        (core,),
        (up, up_oth, own, oth),
        [pl.BlockSpec(block, lambda i, core: (0, 0, 0, core[0]))] + [whole(block)] * 3,
        struct((NB, NB), F32),
        whole((NB, NB)),
        flops=1 << 30,
        moved=2 << 20,
    )


ORDER = (2, 1, 3, 0)
SHARE = HALF // 4


def first_body(x_ref, mid_ref, kown_ref, koth_ref, own_ref, oth_ref, *out_refs):
    total = 0.0
    for rel, (weight, mixed) in enumerate(((kown_ref, own_ref), (koth_ref, oth_ref))):
        grad = mid_ref[:, rel].reshape(SIDE, SHARE).astype(F32) * weight[...].reshape(SIDE, SHARE).astype(F32)
        total = total + lax.dot_general(
            grad.astype(BF),
            mixed[...].reshape(SIDE, WIDTH),
            (((0,), (0,)), ((), ())),
            preferred_element_type=F32,
        )
    for step, ref in enumerate(out_refs):

        @pl.when(pl.program_id(0) == step)
        def _():
            ref[...] = total.astype(ref.dtype)


def first_terms(x, mid, kown, koth, own, oth):
    def chunk(i, x):
        step = jnp.where(i == 0, 2, jnp.where(i == 2, 3, jnp.where(i == 1, 1, 0)))
        return lax.rem(x[0] + step, 4)

    weight = pl.BlockSpec((PEERS, LOCAL, ROWS, SHARE), lambda i, x: (0, 0, 0, chunk(i, x)))
    mixed = whole((PEERS, LOCAL, ROWS, WIDTH))
    out = (SHARE, WIDTH)
    return call(
        first_body,
        (x,),
        (mid, kown, koth, own, oth),
        [pl.BlockSpec((PEERS, 2, LOCAL, ROWS, SHARE), lambda i, x: (0, 0, 0, 0, chunk(i, x))), weight, weight]
        + [mixed, mixed],
        [struct(out), struct(out), struct(out), struct(out, F32)],
        [whole(out)] * 4,
        grid=(4,),
        flops=1 << 30,
        moved=5 << 20,
    )


def grads_body(
    core_ref, mid_ref, got_ref, blocks_ref, kown_ref, koth_ref, in_ref, gate_ref, ff_ref, gin_ref, ggate_ref, gkern_ref
):
    core = core_ref[0]
    own = pl.ds(pl.multiple_of(core * HALF, HALF), HALF)
    oth = pl.ds(pl.multiple_of((1 - core) * HALF, HALF), HALF)
    total = 0.0
    for at, mid, weight in ((own, mid_ref[:, 0], kown_ref), (oth, got_ref[...], koth_ref)):
        mid = mid.astype(F32)
        grad = (mid * blocks_ref[:, :, :, at].astype(F32)).astype(BF)
        for b in range(LOCAL):
            gkern_ref[b, :, at] = grad[:, b].reshape(GROUP * ROWS, HALF)
        grad = (mid * weight[...].astype(F32)).astype(BF).reshape(STEP_ROWS, HALF)
        total = total + jnp.dot(grad, ff_ref[at, :], preferred_element_type=F32)
    total = total.reshape(GROUP, LOCAL, ROWS, WIDTH)
    for b in range(LOCAL):
        grad = total[:, b].reshape(GROUP * ROWS, WIDTH)
        sig = sigmoid(gate_ref[b])
        gin_ref[b] = (grad * sig).astype(BF)
        ggate_ref[b] = (grad * in_ref[b].astype(F32) * sig * (1.0 - sig)).astype(BF)


def grads(core, mid, got, blocks, kown, koth, inputs, gates, ff):
    out = struct((LOCAL, CHANNELS, WIDTH))
    return call(
        grads_body,
        (core,),
        (mid, got, blocks, kown, koth, inputs, gates, ff),
        [
            pl.BlockSpec((GROUP, 1, LOCAL, ROWS, HALF), lambda i, *_: (i, 0, 0, 0, 0)),
            rows_spec(HALF),
            rows_spec(WIDTH),
            rows_spec(HALF),
            rows_spec(HALF),
            natural_spec(),
            natural_spec(),
            whole((WIDTH, WIDTH)),
        ],
        [out, out, out],
        [natural_spec()] * 3,
        grid=(PEERS // GROUP,),
        flops=1 << 30,
        moved=10 << 20,
    )


def join_body(core_ref, mid_ref, got_ref, out_ref):
    core = core_ref[0]
    own = pl.ds(pl.multiple_of(core * HALF, HALF), HALF)
    oth = pl.ds(pl.multiple_of((1 - core) * HALF, HALF), HALF)
    for b in range(LOCAL):
        out_ref[b, :, own] = mid_ref[:, 0, b].reshape(GROUP * ROWS, HALF)
        out_ref[b, :, oth] = got_ref[:, b].reshape(GROUP * ROWS, HALF)


def join(core, mid, got):
    return call(
        join_body,
        (core,),
        (mid, got),
        [pl.BlockSpec((GROUP, 1, LOCAL, ROWS, HALF), lambda i, *_: (i, 0, 0, 0, 0)), rows_spec(HALF)],
        struct((LOCAL, CHANNELS, WIDTH)),
        natural_spec(),
        grid=(PEERS // GROUP,),
        moved=4 << 20,
    )


def on_device(inputs, gates, kernel, first_factor, second_factor, upstream):
    core, x, y = (lax.axis_index(axis) for axis in ("c", "x", "y"))
    core_at, x_at = (value.reshape(1).astype(jnp.int32) for value in (core, x))
    all_channels = CHANNELS * lax.axis_size("zl") * lax.axis_size("x")

    up = exchange(pack(upstream))
    wide, turned = widen(core_at, second_factor)
    mixed, blocks, kern_own, kern_oth, kown, koth = forward(core_at, inputs, gates, kernel, first_factor)
    kern_oth = swap(kern_oth)
    koth_got = swap(koth)
    mixed_got = swap(mixed)

    kern_own = exchange(after(kern_own, up))
    up_oth = swap(lax.dynamic_slice_in_dim(up, (1 - core) * HALF, HALF, 3))
    mid = across(core_at, turned, up, up_oth)
    mid = exchange(after(mid, kern_own))
    kern_oth = exchange(after(kern_oth, mid))
    out = exchange(across(core_at, wide, kern_own, kern_oth))
    output = join(core_at, out, swap(out[:, 1]))

    sent2, sent1, sent3, total = first_terms(x_at, mid, kown, koth_got, mixed, mixed_got)
    got = [shift(sent2, "x", 2), shift(sent1, "x", 1), shift(sent3, "x", 3)]
    total = total + got[1].astype(F32) + got[2].astype(F32) + got[0].astype(F32)
    total = total.reshape(4, SHARE // 4, WIDTH)
    parts = total.astype(BF)
    got = [shift(lax.dynamic_index_in_dim(parts, lax.rem(y + step, 4), 0, False), "y", step) for step in (2, 1, 3)]
    total = lax.dynamic_index_in_dim(total, y, 0, False)
    for part in got:
        total = total + part.astype(F32)
    for axis, bit in (("zl", 1), ("zh", 1), ("zh", 2)):
        part = total.astype(BF)
        total = part.astype(F32) + flip(part, axis, bit).astype(F32)
    total = total * (1.0 / math.sqrt(NB * all_channels))
    grad_first = lax.ppermute(total, AXES, to_owner())

    got = swap(mid[:, 1])
    grad_inputs, grad_gates, grad_kernel = grads(core_at, mid, got, blocks, kown, koth, inputs, gates, first_factor)

    total = second(core_at, up, up_oth, kern_own, kern_oth)
    for axis, bit in (("c", 1), ("x", 1), ("x", 2), ("zl", 1), ("y", 1), ("y", 2), ("zh", 1), ("zh", 2)):
        total = total + flip(total, axis, bit)
    place = (lax.axis_index("zh") * 4 + y) * 2 + core
    grad_second = lax.dynamic_slice_in_dim(total, place * LOCAL, LOCAL, 0)
    grad_second = grad_second * (1.0 / math.sqrt(all_channels * WIDTH))
    return (output, grad_inputs, grad_gates, grad_kernel, grad_first, grad_second)


def solution(mesh):
    fine = Mesh(mesh.devices.reshape(2, 4, 4, 4, 2), AXES)
    seq, dp = ("zh", "y", "c"), ("zl", "x")
    big = P(seq, dp, None)
    return jax.shard_map(
        on_device,
        mesh=fine,
        in_specs=(big, big, big, P(), P(), big),
        out_specs=(big, big, big, big, P(seq, None), P(seq, None)),
        check_vma=False,
    )
```

```python
import math

import jax
import jax.numpy as jnp
from jax import lax
from jax.experimental import pallas as pl
from jax.experimental.pallas import tpu as pltpu
from jax.sharding import Mesh
from jax.sharding import PartitionSpec as P

AXES = ("zl", "x", "zh", "y", "c")
BF = jnp.bfloat16
F32 = jnp.float32
PEERS, LOCAL, ROWS, HALF = 16, 4, 8, 512
CHANNELS, WIDTH = PEERS * ROWS, 2 * HALF
NB = PEERS * 2 * LOCAL
SIDE = PEERS * LOCAL * ROWS
LIMIT = 60 * 1024 * 1024


def swap(value):
    return lax.ppermute(value, "c", [(0, 1), (1, 0)])


def flip(value, axis, bit):
    size = lax.axis_size(axis)
    return lax.ppermute(value, axis, [(i, i ^ bit) for i in range(size)])


def shift(value, axis, step):
    size = lax.axis_size(axis)
    return lax.ppermute(value, axis, [(i, (i + step) % size) for i in range(size)])


def exchange(value):
    return lax.all_to_all(value, ("y", "zh"), 0, 0, tiled=True)


def to_owner(step):
    perm = []
    for zl in range(2):
        for x in range(4):
            for zh in range(4):
                for y in range(4):
                    for c in range(2):
                        place = 16 * c + 4 * x + y
                        source = (((zl * 4 + x) * 4 + zh) * 4 + y) * 2 + c
                        target = (((zl * 4 + (zh ^ step)) * 4 + place // 8) * 4 + place // 2 % 4) * 2 + place % 2
                        perm.append((source, target))
    return perm


def call(body, scalars, operands, in_specs, out_shapes, out_specs, grid=(1,), scratch=()):
    return pl.pallas_call(
        body,
        out_shape=out_shapes,
        grid_spec=pltpu.PrefetchScalarGridSpec(
            num_scalar_prefetch=len(scalars),
            grid=grid,
            in_specs=in_specs,
            out_specs=out_specs,
            scratch_shapes=list(scratch),
        ),
        compiler_params=pltpu.CompilerParams(vmem_limit_bytes=LIMIT),
        cost_estimate=pl.CostEstimate(flops=1 << 10, bytes_accessed=1 << 10, transcendentals=0),
    )(*scalars, *operands)


def whole(shape):
    return pl.BlockSpec(shape, lambda *_: (0,) * len(shape))


def struct(shape, dtype=BF):
    return jax.ShapeDtypeStruct(shape, dtype)


def sigmoid(gates):
    return jax.nn.sigmoid(gates.astype(F32))


def pack_body(in_ref, out_ref):
    for b in range(LOCAL):
        out_ref[:, b] = in_ref[b].reshape(PEERS, ROWS, WIDTH)


def pack(value):
    return call(
        pack_body,
        (),
        (value,),
        [whole((LOCAL, CHANNELS, WIDTH))],
        struct((PEERS, LOCAL, ROWS, WIDTH)),
        whole((PEERS, LOCAL, ROWS, WIDTH)),
    )


def placed(n, core):
    rel = n // SIDE
    real = rel + core - 2 * rel * core
    peer = (n // (LOCAL * ROWS)) % PEERS
    return (peer % 4 * 4 + peer // 4) * (2 * LOCAL) + real * LOCAL + (n // ROWS) % LOCAL


def widen_body(at_ref, sf_ref, wide_ref, turned_ref):
    core = at_ref[0]
    size = 2 * SIDE
    n = lax.broadcasted_iota(jnp.int32, (size, NB), 0)
    o = lax.broadcasted_iota(jnp.int32, (size, NB), 1)
    pick = jnp.where(placed(n, core) == o, 1.0, 0.0).astype(BF)
    row = lax.broadcasted_iota(jnp.int32, (size, size), 0) % ROWS
    column = lax.broadcasted_iota(jnp.int32, (size, size), 1) % ROWS
    same = row == column
    for ref, dim in ((wide_ref, 0), (turned_ref, 1)):
        tall = lax.dot_general(pick, sf_ref[...], (((1,), (dim,)), ((), ())), preferred_element_type=F32)
        full = lax.dot_general(tall.astype(BF), pick, (((1,), (1,)), ((), ())), preferred_element_type=F32)
        ref[...] = jnp.where(same, full, 0.0).astype(BF)


def widen(at, sf):
    shape = (2 * SIDE, 2 * SIDE)
    return call(
        widen_body,
        (at,),
        (sf,),
        [whole((NB, NB))],
        [struct(shape), struct(shape)],
        [whole(shape), whole(shape)],
    )


GROUP = 4
STEP_ROWS = GROUP * LOCAL * ROWS


def forward_body(
    core_ref, in_ref, gate_ref, kernel_ref, ff_ref, mixed_ref, blocks_ref, own_ref, oth_ref, kown_ref, koth_ref, flat
):
    core = core_ref[0]
    for b in range(LOCAL):
        mixed = (in_ref[b].astype(F32) * sigmoid(gate_ref[b])).astype(BF)
        for g in range(GROUP):
            piece = mixed[g * ROWS : (g + 1) * ROWS]
            mixed_ref[g, b] = piece
            flat[(g * LOCAL + b) * ROWS : (g * LOCAL + b + 1) * ROWS] = piece
    blocks = lax.dot_general(flat[...], ff_ref[...], (((1,), (1,)), ((), ())), preferred_element_type=F32)
    blocks = blocks.astype(BF).reshape(GROUP, LOCAL, ROWS, WIDTH)
    blocks_ref[...] = blocks
    for b in range(LOCAL):
        weight = kernel_ref[b].reshape(GROUP, ROWS, WIDTH)
        kern = (blocks[:, b].astype(F32) * weight.astype(F32)).astype(BF)
        low, high = kern[..., :HALF], kern[..., HALF:]
        own_ref[:, b] = jnp.where(core == 0, low, high)
        oth_ref[:, b] = jnp.where(core == 0, high, low)
        low, high = weight[..., :HALF], weight[..., HALF:]
        kown_ref[:, b] = jnp.where(core == 0, low, high)
        koth_ref[:, b] = jnp.where(core == 0, high, low)


def natural_spec():
    return pl.BlockSpec((LOCAL, GROUP * ROWS, WIDTH), lambda i, *_: (0, i, 0))


def rows_spec(width):
    return pl.BlockSpec((GROUP, LOCAL, ROWS, width), lambda i, *_: (i, 0, 0, 0))


def forward(core, inputs, gates, kernel, ff):
    full, part = struct((PEERS, LOCAL, ROWS, WIDTH)), struct((PEERS, LOCAL, ROWS, HALF))
    return call(
        forward_body,
        (core,),
        (inputs, gates, kernel, ff),
        [natural_spec()] * 3 + [whole((WIDTH, WIDTH))],
        [full, full, part, part, part, part],
        [rows_spec(WIDTH)] * 2 + [rows_spec(HALF)] * 4,
        grid=(PEERS // GROUP,),
        scratch=[pltpu.VMEM((STEP_ROWS, WIDTH), BF)],
    )


CHUNK = 256


STEPS = HALF // CHUNK


def across_body(at_ref, wide_ref, own_ref, oth_ref, out_ref):
    own = own_ref[...].reshape(SIDE, CHUNK)
    oth = oth_ref[...].reshape(SIDE, CHUNK)
    total = jnp.dot(wide_ref[:, :SIDE], own, preferred_element_type=F32)
    total = total + jnp.dot(wide_ref[:, SIDE:], oth, preferred_element_type=F32)
    total = total.astype(BF)
    for rel in range(2):
        out_ref[:, rel] = total[rel * SIDE : (rel + 1) * SIDE].reshape(PEERS, LOCAL, ROWS, CHUNK)


def across(at, wide, own, oth, own_spec, oth_spec):
    return call(
        across_body,
        (at,),
        (wide, own, oth),
        [whole((2 * SIDE, 2 * SIDE)), own_spec, oth_spec],
        struct((PEERS, 2, LOCAL, ROWS, HALF)),
        pl.BlockSpec((PEERS, 2, LOCAL, ROWS, CHUNK), lambda i, at: (0, 0, 0, 0, i)),
        grid=(STEPS,),
    )


def across_up(at, wide, up, up_oth):
    block = (PEERS, LOCAL, ROWS, CHUNK)
    own = pl.BlockSpec(block, lambda i, at: (0, 0, 0, at[0] * STEPS + i))
    return across(at, wide, up, up_oth, own, pl.BlockSpec(block, lambda i, at: (0, 0, 0, i)))


def across_kern(at, wide, kern):
    block = (PEERS, 1, LOCAL, ROWS, CHUNK)
    own = pl.BlockSpec(block, lambda i, at: (0, 0, 0, 0, i))
    return across(at, wide, kern, kern, own, pl.BlockSpec(block, lambda i, at: (0, 1, 0, 0, i)))


def second_body(at_ref, up_ref, up_oth_ref, kern_ref, out_ref):
    core = at_ref[0]
    row = lax.broadcasted_iota(jnp.int32, (SIDE, SIDE), 0) % ROWS
    column = lax.broadcasted_iota(jnp.int32, (SIDE, SIDE), 1) % ROWS
    same = row == column
    tall = []
    for ref in (up_ref, up_oth_ref):
        up = ref[...].reshape(SIDE, HALF)
        wide = []
        for rel in range(2):
            kern = kern_ref[:, rel].reshape(SIDE, HALF)
            full = lax.dot_general(up, kern, (((1,), (1,)), ((), ())), preferred_element_type=F32)
            wide.append(jnp.where(same, full, 0.0).reshape(SIDE // ROWS, ROWS, SIDE).sum(1))
        tall.append(jnp.concatenate(wide, 1))
    tall = jnp.concatenate(tall, 0)
    n = lax.broadcasted_iota(jnp.int32, (2 * SIDE, NB), 0)
    o = lax.broadcasted_iota(jnp.int32, (2 * SIDE, NB), 1)
    pick = jnp.where(placed(n, core) == o, 1.0, 0.0)
    total = jnp.dot(tall, pick, precision=lax.Precision.HIGHEST, preferred_element_type=F32)
    n = lax.broadcasted_iota(jnp.int32, (NB, NB), 1) * ROWS
    o = lax.broadcasted_iota(jnp.int32, (NB, NB), 0)
    pick = jnp.where(placed(n, core) == o, 1.0, 0.0)
    out_ref[...] = jnp.dot(pick, total, precision=lax.Precision.HIGHEST, preferred_element_type=F32)


def second(at, up, up_oth, kern):
    block = (PEERS, LOCAL, ROWS, HALF)
    return call(
        second_body,
        (at,),
        (up, up_oth, kern),
        [pl.BlockSpec(block, lambda i, at: (0, 0, 0, at[0])), whole(block), whole(kern.shape)],
        struct((NB, NB), F32),
        whole((NB, NB)),
    )


SHARE = HALF // 4
PACKED = WIDTH + NB


def first_body(x_ref, core_ref, mid_ref, kown_ref, koth_ref, own_ref, oth_ref, second_ref, *out_refs):
    total = 0.0
    for rel, (weight, mixed) in enumerate(((kown_ref, own_ref), (koth_ref, oth_ref))):
        grad = mid_ref[:, rel].reshape(SIDE, SHARE) * weight[...].reshape(SIDE, SHARE)
        total = total + lax.dot_general(
            grad,
            mixed[...].reshape(SIDE, WIDTH),
            (((0,), (0,)), ((), ())),
            preferred_element_type=F32,
        )
    chunk = lax.rem(x_ref[0] + turn(pl.program_id(0)), 4)
    terms = second_ref[pl.ds(pl.multiple_of(core_ref[0] * (NB // 2) + chunk * (NB // 8), NB // 8), NB // 8), :]
    blank = jnp.zeros((SHARE // 4 - LOCAL, NB), F32)
    terms = [piece for y in range(4) for piece in (terms[y * LOCAL : (y + 1) * LOCAL], blank)]
    terms = jnp.concatenate(terms, 0)
    for step, ref in enumerate(out_refs):

        @pl.when(pl.program_id(0) == step)
        def _():
            ref[:, :WIDTH] = total.astype(ref.dtype)
            ref[:, WIDTH:] = terms.astype(ref.dtype)


def turn(i):
    return jnp.where(i == 0, 2, jnp.where(i == 2, 3, jnp.where(i == 1, 1, 0)))


def first_terms(x, core, mid, kown, koth, own, oth, terms):
    def chunk(i, x):
        return lax.rem(x[0] + turn(i), 4)

    weight = pl.BlockSpec((PEERS, LOCAL, ROWS, SHARE), lambda i, x, core: (0, 0, 0, chunk(i, x)))
    mixed = whole((PEERS, LOCAL, ROWS, WIDTH))
    out = (SHARE, PACKED)
    return call(
        first_body,
        (x, core),
        (mid, kown, koth, own, oth, terms),
        [pl.BlockSpec((PEERS, 2, LOCAL, ROWS, SHARE), lambda i, x, core: (0, 0, 0, 0, chunk(i, x))), weight, weight]
        + [mixed, mixed, whole((NB, NB))],
        [struct(out), struct(out), struct(out), struct(out, F32)],
        [whole(out)] * 4,
        grid=(4,),
    )


def grads_body(
    core_ref, mid_ref, got_ref, blocks_ref, kown_ref, koth_ref, in_ref, gate_ref, ff_ref, gin_ref, ggate_ref, gkern_ref
):
    core = core_ref[0]
    own = pl.ds(pl.multiple_of(core * HALF, HALF), HALF)
    oth = pl.ds(pl.multiple_of((1 - core) * HALF, HALF), HALF)
    total = 0.0
    for at, mid, weight in ((own, mid_ref[:, 0], kown_ref), (oth, got_ref[...], koth_ref)):
        grad = mid * blocks_ref[:, :, :, at]
        for b in range(LOCAL):
            gkern_ref[b, :, at] = grad[:, b].reshape(GROUP * ROWS, HALF)
        grad = (mid * weight[...]).reshape(STEP_ROWS, HALF)
        total = total + jnp.dot(grad, ff_ref[at, :], preferred_element_type=F32)
    total = total.reshape(GROUP, LOCAL, ROWS, WIDTH)
    for b in range(LOCAL):
        grad = total[:, b].reshape(GROUP * ROWS, WIDTH)
        sig = sigmoid(gate_ref[b])
        gin_ref[b] = (grad * sig).astype(BF)
        ggate_ref[b] = (grad * in_ref[b].astype(F32) * sig * (1.0 - sig)).astype(BF)


def grads(core, mid, got, blocks, kown, koth, inputs, gates, ff):
    out = struct((LOCAL, CHANNELS, WIDTH))
    return call(
        grads_body,
        (core,),
        (mid, got, blocks, kown, koth, inputs, gates, ff),
        [
            pl.BlockSpec((GROUP, 1, LOCAL, ROWS, HALF), lambda i, *_: (i, 0, 0, 0, 0)),
            rows_spec(HALF),
            rows_spec(WIDTH),
            rows_spec(HALF),
            rows_spec(HALF),
            natural_spec(),
            natural_spec(),
            whole((WIDTH, WIDTH)),
        ],
        [out, out, out],
        [natural_spec()] * 3,
        grid=(PEERS // GROUP,),
    )


def join_body(core_ref, mid_ref, got_ref, out_ref):
    core = core_ref[0]
    own = pl.ds(pl.multiple_of(core * HALF, HALF), HALF)
    oth = pl.ds(pl.multiple_of((1 - core) * HALF, HALF), HALF)
    for b in range(LOCAL):
        out_ref[b, :, own] = mid_ref[:, 0, b].reshape(GROUP * ROWS, HALF)
        out_ref[b, :, oth] = got_ref[:, b].reshape(GROUP * ROWS, HALF)


def join(core, mid, got):
    return call(
        join_body,
        (core,),
        (mid, got),
        [pl.BlockSpec((GROUP, 1, LOCAL, ROWS, HALF), lambda i, *_: (i, 0, 0, 0, 0)), rows_spec(HALF)],
        struct((LOCAL, CHANNELS, WIDTH)),
        natural_spec(),
        grid=(PEERS // GROUP,),
    )


def on_device(inputs, gates, kernel, first_factor, second_factor, upstream):
    core, x, y = (lax.axis_index(axis).astype(jnp.int32) for axis in ("c", "x", "y"))
    x_at, at = x.reshape(1), core.reshape(1)
    all_channels = CHANNELS * lax.axis_size("zl") * lax.axis_size("x")

    up = exchange(pack(upstream))
    mixed, blocks, kern_own, kern_oth, kown, koth = forward(at, inputs, gates, kernel, first_factor)
    kern = jnp.stack([kern_own, swap(kern_oth)], 1)
    wide, turned = widen(at, second_factor)
    up, kern, wide, turned = lax.optimization_barrier((up, kern, wide, turned))

    kern = exchange(kern)
    up_oth = swap(lax.dynamic_slice_in_dim(up, (1 - core) * HALF, HALF, 3))
    mid = across_up(at, turned, up, up_oth)
    koth_got = swap(koth)
    mixed_got = swap(mixed)
    mid, kern, koth_got, mixed_got = lax.optimization_barrier((mid, kern, koth_got, mixed_got))

    mid = exchange(mid)
    out = across_kern(at, wide, kern)

    terms = second(at, up, up_oth, kern)
    terms = terms + swap(terms)
    mid, out, terms = lax.optimization_barrier((mid, out, terms))
    out = exchange(out)

    sent2, sent1, sent3, total = first_terms(x_at, at, mid, kown, koth_got, mixed, mixed_got, terms)
    got = [shift(sent2, "x", 2), shift(sent1, "x", 1), shift(sent3, "x", 3)]
    mid_got = swap(mid[:, 1])
    others = grads(at, mid, mid_got, blocks, kown, koth, inputs, gates, first_factor)
    total, *others = lax.optimization_barrier((total, *others))

    total = total + got[1].astype(F32) + got[2].astype(F32) + got[0].astype(F32)
    total = total.reshape(4, SHARE // 4, PACKED)
    parts = total.astype(BF)
    got = [shift(lax.dynamic_index_in_dim(parts, lax.rem(y + step, 4), 0, False), "y", step) for step in (2, 1, 3)]
    total = lax.dynamic_index_in_dim(total, y, 0, False)
    for part in got:
        total = total + part.astype(F32)
    part = total.astype(BF)
    near = flip(part, "zl", 1)
    output = join(at, out, swap(out[:, 1]))
    part, output = lax.optimization_barrier((part, output))
    part = (part.astype(F32) + near.astype(F32)).astype(BF)
    got = [lax.ppermute(part, AXES, to_owner(step)).astype(F32) for step in range(4)]
    total = (got[0] + got[1]) + (got[2] + got[3])
    grad_first = total[:, :WIDTH] * (1.0 / math.sqrt(NB * all_channels))
    grad_second = total[:LOCAL, WIDTH:] * (1.0 / math.sqrt(all_channels * WIDTH))
    return (output, *others, grad_first, grad_second)


def solution(mesh):
    fine = Mesh(mesh.devices.reshape(2, 4, 4, 4, 2), AXES)
    seq, dp = ("zh", "y", "c"), ("zl", "x")
    big = P(seq, dp, None)
    return jax.shard_map(
        on_device,
        mesh=fine,
        in_specs=(big, big, big, P(), P(), big),
        out_specs=(big, big, big, big, P(seq, None), P(seq, None)),
        check_vma=False,
    )
```

```python
import math

import jax
import jax.numpy as jnp
from jax import lax
from jax.experimental import pallas as pl
from jax.experimental.pallas import tpu as pltpu
from jax.sharding import Mesh
from jax.sharding import PartitionSpec as P

AXES = ("zl", "x", "zh", "y", "c")
BF = jnp.bfloat16
F32 = jnp.float32
PEERS, LOCAL, ROWS, HALF = 16, 4, 8, 512
CHANNELS, WIDTH = PEERS * ROWS, 2 * HALF
NB = PEERS * 2 * LOCAL
SIDE = PEERS * LOCAL * ROWS
LIMIT = 60 * 1024 * 1024


def swap(value):
    return lax.ppermute(value, "c", [(0, 1), (1, 0)])


def flip(value, axis, bit):
    size = lax.axis_size(axis)
    return lax.ppermute(value, axis, [(i, i ^ bit) for i in range(size)])


def shift(value, axis, step):
    size = lax.axis_size(axis)
    return lax.ppermute(value, axis, [(i, (i + step) % size) for i in range(size)])


def exchange(value):
    return lax.all_to_all(value, ("y", "zh"), 0, 0, tiled=True)


def to_owner(step):
    perm = []
    for zl in range(2):
        for x in range(4):
            for zh in range(4):
                for y in range(4):
                    for c in range(2):
                        place = (2 * c + x // 2) * 8 + 2 * y + x % 2
                        source = (((zl * 4 + x) * 4 + zh) * 4 + y) * 2 + c
                        target = (((zl * 4 + (zh ^ step)) * 4 + place // 8) * 4 + place // 2 % 4) * 2 + place % 2
                        perm.append((source, target))
    return perm


def call(body, scalars, operands, in_specs, out_shapes, out_specs, grid=(1,), scratch=()):
    return pl.pallas_call(
        body,
        out_shape=out_shapes,
        grid_spec=pltpu.PrefetchScalarGridSpec(
            num_scalar_prefetch=len(scalars),
            grid=grid,
            in_specs=in_specs,
            out_specs=out_specs,
            scratch_shapes=list(scratch),
        ),
        compiler_params=pltpu.CompilerParams(vmem_limit_bytes=LIMIT),
        cost_estimate=pl.CostEstimate(flops=1 << 10, bytes_accessed=1 << 10, transcendentals=0),
    )(*scalars, *operands)


def whole(shape):
    return pl.BlockSpec(shape, lambda *_: (0,) * len(shape))


def struct(shape, dtype=BF):
    return jax.ShapeDtypeStruct(shape, dtype)


def sigmoid(gates):
    return jax.nn.sigmoid(gates.astype(F32))


def pack_body(in_ref, out_ref):
    for b in range(LOCAL):
        out_ref[:, b] = in_ref[b].reshape(PEERS, ROWS, WIDTH)


def pack(value):
    return call(
        pack_body,
        (),
        (value,),
        [whole((LOCAL, CHANNELS, WIDTH))],
        struct((PEERS, LOCAL, ROWS, WIDTH)),
        whole((PEERS, LOCAL, ROWS, WIDTH)),
    )


def placed(n, core):
    rel = n // SIDE
    real = rel + core - 2 * rel * core
    peer = (n // (LOCAL * ROWS)) % PEERS
    return (peer % 4 * 4 + peer // 4) * (2 * LOCAL) + real * LOCAL + (n // ROWS) % LOCAL


def widen_body(at_ref, sf_ref, wide_ref, turned_ref):
    core = at_ref[0]
    size = 2 * SIDE
    n = lax.broadcasted_iota(jnp.int32, (size, NB), 0)
    o = lax.broadcasted_iota(jnp.int32, (size, NB), 1)
    pick = jnp.where(placed(n, core) == o, 1.0, 0.0).astype(BF)
    row = lax.broadcasted_iota(jnp.int32, (size, size), 0) % ROWS
    column = lax.broadcasted_iota(jnp.int32, (size, size), 1) % ROWS
    same = row == column
    for ref, dim in ((wide_ref, 0), (turned_ref, 1)):
        tall = lax.dot_general(pick, sf_ref[...], (((1,), (dim,)), ((), ())), preferred_element_type=F32)
        full = lax.dot_general(tall.astype(BF), pick, (((1,), (1,)), ((), ())), preferred_element_type=F32)
        ref[...] = jnp.where(same, full, 0.0).astype(BF)


def widen(at, sf):
    shape = (2 * SIDE, 2 * SIDE)
    return call(
        widen_body,
        (at,),
        (sf,),
        [whole((NB, NB))],
        [struct(shape), struct(shape)],
        [whole(shape), whole(shape)],
    )


GROUP = 8
STEP_ROWS = GROUP * LOCAL * ROWS


def forward_body(
    core_ref, in_ref, gate_ref, kernel_ref, ff_ref, mixed_ref, blocks_ref, own_ref, oth_ref, kown_ref, koth_ref, flat
):
    core = core_ref[0]
    for b in range(LOCAL):
        mixed = (in_ref[b].astype(F32) * sigmoid(gate_ref[b])).astype(BF)
        for g in range(GROUP):
            piece = mixed[g * ROWS : (g + 1) * ROWS]
            mixed_ref[g, b] = piece
            flat[(g * LOCAL + b) * ROWS : (g * LOCAL + b + 1) * ROWS] = piece
    blocks = lax.dot_general(flat[...], ff_ref[...], (((1,), (1,)), ((), ())), preferred_element_type=F32)
    blocks = blocks.astype(BF).reshape(GROUP, LOCAL, ROWS, WIDTH)
    blocks_ref[...] = blocks
    for b in range(LOCAL):
        weight = kernel_ref[b].reshape(GROUP, ROWS, WIDTH)
        kern = (blocks[:, b].astype(F32) * weight.astype(F32)).astype(BF)
        low, high = kern[..., :HALF], kern[..., HALF:]
        own_ref[:, b] = jnp.where(core == 0, low, high)
        oth_ref[:, b] = jnp.where(core == 0, high, low)
        low, high = weight[..., :HALF], weight[..., HALF:]
        kown_ref[:, b] = jnp.where(core == 0, low, high)
        koth_ref[:, b] = jnp.where(core == 0, high, low)


def natural_spec():
    return pl.BlockSpec((LOCAL, GROUP * ROWS, WIDTH), lambda i, *_: (0, i, 0))


def rows_spec(width):
    return pl.BlockSpec((GROUP, LOCAL, ROWS, width), lambda i, *_: (i, 0, 0, 0))


def forward(core, inputs, gates, kernel, ff):
    full, part = struct((PEERS, LOCAL, ROWS, WIDTH)), struct((PEERS, LOCAL, ROWS, HALF))
    return call(
        forward_body,
        (core,),
        (inputs, gates, kernel, ff),
        [natural_spec()] * 3 + [whole((WIDTH, WIDTH))],
        [full, full, part, part, part, part],
        [rows_spec(WIDTH)] * 2 + [rows_spec(HALF)] * 4,
        grid=(PEERS // GROUP,),
        scratch=[pltpu.VMEM((STEP_ROWS, WIDTH), BF)],
    )


CHUNK = 256


STEPS = HALF // CHUNK


def across_body(at_ref, wide_ref, own_ref, oth_ref, out_ref):
    own = own_ref[...].reshape(SIDE, CHUNK)
    oth = oth_ref[...].reshape(SIDE, CHUNK)
    total = jnp.dot(wide_ref[:, :SIDE], own, preferred_element_type=F32)
    total = total + jnp.dot(wide_ref[:, SIDE:], oth, preferred_element_type=F32)
    total = total.astype(BF)
    for rel in range(2):
        out_ref[:, rel] = total[rel * SIDE : (rel + 1) * SIDE].reshape(PEERS, LOCAL, ROWS, CHUNK)


def across(at, wide, own, oth, own_spec, oth_spec):
    return call(
        across_body,
        (at,),
        (wide, own, oth),
        [whole((2 * SIDE, 2 * SIDE)), own_spec, oth_spec],
        struct((PEERS, 2, LOCAL, ROWS, HALF)),
        pl.BlockSpec((PEERS, 2, LOCAL, ROWS, CHUNK), lambda i, at: (0, 0, 0, 0, i)),
        grid=(STEPS,),
    )


def across_up(at, wide, up, up_oth):
    block = (PEERS, LOCAL, ROWS, CHUNK)
    own = pl.BlockSpec(block, lambda i, at: (0, 0, 0, at[0] * STEPS + i))
    return across(at, wide, up, up_oth, own, pl.BlockSpec(block, lambda i, at: (0, 0, 0, i)))


def across_kern(at, wide, kern):
    block = (PEERS, 1, LOCAL, ROWS, CHUNK)
    own = pl.BlockSpec(block, lambda i, at: (0, 0, 0, 0, i))
    return across(at, wide, kern, kern, own, pl.BlockSpec(block, lambda i, at: (0, 1, 0, 0, i)))


def second_body(at_ref, up_ref, up_oth_ref, kern_ref, out_ref):
    core = at_ref[0]
    row = lax.broadcasted_iota(jnp.int32, (SIDE, SIDE), 0) % ROWS
    column = lax.broadcasted_iota(jnp.int32, (SIDE, SIDE), 1) % ROWS
    same = row == column
    tall = []
    for ref in (up_ref, up_oth_ref):
        up = ref[...].reshape(SIDE, HALF)
        wide = []
        for rel in range(2):
            kern = kern_ref[:, rel].reshape(SIDE, HALF)
            full = lax.dot_general(up, kern, (((1,), (1,)), ((), ())), preferred_element_type=F32)
            wide.append(jnp.where(same, full, 0.0).reshape(SIDE // ROWS, ROWS, SIDE).sum(1))
        tall.append(jnp.concatenate(wide, 1))
    tall = jnp.concatenate(tall, 0)
    n = lax.broadcasted_iota(jnp.int32, (2 * SIDE, NB), 0)
    o = lax.broadcasted_iota(jnp.int32, (2 * SIDE, NB), 1)
    pick = jnp.where(placed(n, core) == o, 1.0, 0.0)
    total = jnp.dot(tall, pick, precision=lax.Precision.HIGHEST, preferred_element_type=F32)
    n = lax.broadcasted_iota(jnp.int32, (NB, NB), 1) * ROWS
    o = lax.broadcasted_iota(jnp.int32, (NB, NB), 0)
    pick = jnp.where(placed(n, core) == o, 1.0, 0.0)
    out_ref[...] = jnp.dot(pick, total, precision=lax.Precision.HIGHEST, preferred_element_type=F32)


def second(at, up, up_oth, kern):
    block = (PEERS, LOCAL, ROWS, HALF)
    return call(
        second_body,
        (at,),
        (up, up_oth, kern),
        [pl.BlockSpec(block, lambda i, at: (0, 0, 0, at[0])), whole(block), whole(kern.shape)],
        struct((NB, NB), F32),
        whole((NB, NB)),
    )


SHARE = HALF // 4
PACKED = WIDTH + NB


def first_body(x_ref, at_ref, mid_ref, kown_ref, koth_ref, own_ref, oth_ref, second_ref, *refs):
    total = 0.0
    for rel, (weight, mixed) in enumerate(((kown_ref, own_ref), (koth_ref, oth_ref))):
        grad = mid_ref[:, rel].reshape(SIDE, HALF) * weight[...].reshape(SIDE, HALF)
        total = total + lax.dot_general(
            grad, mixed[...].reshape(SIDE, WIDTH), (((0,), (0,)), ((), ())), preferred_element_type=F32
        )
    full_ref = refs[4]
    full_ref[...] = total
    row = lax.broadcasted_iota(jnp.int32, (SHARE, NB), 0)
    column = lax.broadcasted_iota(jnp.int32, (SHARE, NB), 1)
    for step, ref in zip((2, 1, 3, 0), refs):
        x = lax.rem(x_ref[0] + step, 4)
        high, low = x // 2, lax.rem(x, 2)
        for y in range(4):
            rows = pl.ds(pl.multiple_of((high * 8 + 2 * y + low) * 32, 32), 32)
            ref[y * 32 : (y + 1) * 32, :WIDTH] = full_ref[rows, :].astype(ref.dtype)
        place = (2 * at_ref[0] + high) * 8 + row // 32 * 2 + low
        pick = jnp.where((place * LOCAL + row % 32 == column) & (row % 32 < LOCAL), 1.0, 0.0)
        terms = jnp.dot(pick, second_ref[...], precision=lax.Precision.HIGHEST, preferred_element_type=F32)
        ref[:, WIDTH:] = terms.astype(ref.dtype)


def first_terms(x, at, mid, kown, koth, own, oth, terms):
    out = (SHARE, PACKED)
    operands = (mid, kown, koth, own, oth, terms)
    return call(
        first_body,
        (x, at),
        operands,
        [whole(operand.shape) for operand in operands],
        [struct(out), struct(out), struct(out), struct(out, F32)],
        [whole(out)] * 4,
        scratch=[pltpu.VMEM((HALF, WIDTH), F32)],
    )


def grads_body(
    core_ref, mid_ref, got_ref, blocks_ref, kown_ref, koth_ref, in_ref, gate_ref, ff_ref, gin_ref, ggate_ref, gkern_ref
):
    core = core_ref[0]
    own = pl.ds(pl.multiple_of(core * HALF, HALF), HALF)
    oth = pl.ds(pl.multiple_of((1 - core) * HALF, HALF), HALF)
    total = 0.0
    for at, mid, weight in ((own, mid_ref[:, 0], kown_ref), (oth, got_ref[...], koth_ref)):
        grad = mid * blocks_ref[:, :, :, at]
        for b in range(LOCAL):
            gkern_ref[b, :, at] = grad[:, b].reshape(GROUP * ROWS, HALF)
        grad = (mid * weight[...]).reshape(STEP_ROWS, HALF)
        total = total + jnp.dot(grad, ff_ref[at, :], preferred_element_type=F32)
    total = total.reshape(GROUP, LOCAL, ROWS, WIDTH)
    for b in range(LOCAL):
        grad = total[:, b].reshape(GROUP * ROWS, WIDTH)
        sig = sigmoid(gate_ref[b])
        gin_ref[b] = (grad * sig).astype(BF)
        ggate_ref[b] = (grad * in_ref[b].astype(F32) * sig * (1.0 - sig)).astype(BF)


def grads(core, mid, got, blocks, kown, koth, inputs, gates, ff):
    out = struct((LOCAL, CHANNELS, WIDTH))
    return call(
        grads_body,
        (core,),
        (mid, got, blocks, kown, koth, inputs, gates, ff),
        [
            pl.BlockSpec((GROUP, 1, LOCAL, ROWS, HALF), lambda i, *_: (i, 0, 0, 0, 0)),
            rows_spec(HALF),
            rows_spec(WIDTH),
            rows_spec(HALF),
            rows_spec(HALF),
            natural_spec(),
            natural_spec(),
            whole((WIDTH, WIDTH)),
        ],
        [out, out, out],
        [natural_spec()] * 3,
        grid=(PEERS // GROUP,),
    )


def join_body(core_ref, mid_ref, got_ref, out_ref):
    core = core_ref[0]
    own = pl.ds(pl.multiple_of(core * HALF, HALF), HALF)
    oth = pl.ds(pl.multiple_of((1 - core) * HALF, HALF), HALF)
    for b in range(LOCAL):
        out_ref[b, :, own] = mid_ref[:, 0, b].reshape(GROUP * ROWS, HALF)
        out_ref[b, :, oth] = got_ref[:, b].reshape(GROUP * ROWS, HALF)


def join(core, mid, got):
    return call(
        join_body,
        (core,),
        (mid, got),
        [pl.BlockSpec((GROUP, 1, LOCAL, ROWS, HALF), lambda i, *_: (i, 0, 0, 0, 0)), rows_spec(HALF)],
        struct((LOCAL, CHANNELS, WIDTH)),
        natural_spec(),
        grid=(PEERS // GROUP,),
    )


def on_device(inputs, gates, kernel, first_factor, second_factor, upstream):
    core, x, y = (lax.axis_index(axis).astype(jnp.int32) for axis in ("c", "x", "y"))
    x_at, at = x.reshape(1), core.reshape(1)
    all_channels = CHANNELS * lax.axis_size("zl") * lax.axis_size("x")

    up = exchange(pack(upstream))
    mixed, blocks, kern_own, kern_oth, kown, koth = forward(at, inputs, gates, kernel, first_factor)
    kern = jnp.stack([kern_own, swap(kern_oth)], 1)
    wide, turned = widen(at, second_factor)
    up, kern, wide, turned = lax.optimization_barrier((up, kern, wide, turned))

    kern = exchange(kern)
    up_oth = swap(lax.dynamic_slice_in_dim(up, (1 - core) * HALF, HALF, 3))
    mid = across_up(at, turned, up, up_oth)
    koth_got = swap(koth)
    mixed_got = swap(mixed)
    mid, kern, koth_got, mixed_got = lax.optimization_barrier((mid, kern, koth_got, mixed_got))

    mid = exchange(mid)
    out = across_kern(at, wide, kern)

    terms = second(at, up, up_oth, kern)
    terms = terms + swap(terms)
    mid, out, terms = lax.optimization_barrier((mid, out, terms))
    out = exchange(out)

    sent2, sent1, sent3, total = first_terms(x_at, at, mid, kown, koth_got, mixed, mixed_got, terms)
    got = [shift(sent2, "x", 2), shift(sent1, "x", 1), shift(sent3, "x", 3)]
    mid_got = swap(mid[:, 1])
    others = grads(at, mid, mid_got, blocks, kown, koth, inputs, gates, first_factor)
    total, *others = lax.optimization_barrier((total, *others))

    total = total + got[1].astype(F32) + got[2].astype(F32) + got[0].astype(F32)
    total = total.reshape(4, SHARE // 4, PACKED)
    parts = total.astype(BF)
    got = [shift(lax.dynamic_index_in_dim(parts, lax.rem(y + step, 4), 0, False), "y", step) for step in (2, 1, 3)]
    total = lax.dynamic_index_in_dim(total, y, 0, False)
    for part in got:
        total = total + part.astype(F32)
    part = total.astype(BF)
    near = flip(part, "zl", 1)
    output = join(at, out, swap(out[:, 1]))
    part, output = lax.optimization_barrier((part, output))
    part = (part.astype(F32) + near.astype(F32)).astype(BF)
    got = [lax.ppermute(part, AXES, to_owner(step)).astype(F32) for step in range(4)]
    total = (got[0] + got[1]) + (got[2] + got[3])
    grad_first = total[:, :WIDTH] * (1.0 / math.sqrt(NB * all_channels))
    grad_second = total[:LOCAL, WIDTH:] * (1.0 / math.sqrt(all_channels * WIDTH))
    return (output, *others, grad_first, grad_second)


def solution(mesh):
    fine = Mesh(mesh.devices.reshape(2, 4, 4, 4, 2), AXES)
    seq, dp = ("zh", "y", "c"), ("zl", "x")
    big = P(seq, dp, None)
    return jax.shard_map(
        on_device,
        mesh=fine,
        in_specs=(big, big, big, P(), P(), big),
        out_specs=(big, big, big, big, P(seq, None), P(seq, None)),
        check_vma=False,
    )
```

```python
import math

import jax
import jax.numpy as jnp
from jax import lax
from jax.experimental import pallas as pl
from jax.experimental.pallas import tpu as pltpu
from jax.sharding import Mesh
from jax.sharding import PartitionSpec as P

AXES = ("zl", "x", "zh", "y", "c")
BF = jnp.bfloat16
F32 = jnp.float32
PEERS, LOCAL, ROWS, HALF = 16, 4, 8, 512
CHANNELS, WIDTH = PEERS * ROWS, 2 * HALF
NB = PEERS * 2 * LOCAL
SIDE = PEERS * LOCAL * ROWS
LIMIT = 60 * 1024 * 1024


def swap(value):
    return lax.ppermute(value, "c", [(0, 1), (1, 0)])


def flip(value, axis, bit):
    size = lax.axis_size(axis)
    return lax.ppermute(value, axis, [(i, i ^ bit) for i in range(size)])


def shift(value, axis, step):
    size = lax.axis_size(axis)
    return lax.ppermute(value, axis, [(i, (i + step) % size) for i in range(size)])


def exchange(value):
    return lax.all_to_all(value, ("y", "zh"), 0, 0, tiled=True)


def to_owner(step):
    perm = []
    for zl in range(2):
        for x in range(4):
            for zh in range(4):
                for y in range(4):
                    for c in range(2):
                        place = (2 * c + x // 2) * 8 + 2 * y + x % 2
                        source = (((zl * 4 + x) * 4 + zh) * 4 + y) * 2 + c
                        target = (((zl * 4 + (zh ^ step)) * 4 + place // 8) * 4 + place // 2 % 4) * 2 + place % 2
                        perm.append((source, target))
    return perm


def call(body, scalars, operands, in_specs, out_shapes, out_specs, grid=(1,), scratch=(), limit=LIMIT):
    return pl.pallas_call(
        body,
        out_shape=out_shapes,
        grid_spec=pltpu.PrefetchScalarGridSpec(
            num_scalar_prefetch=len(scalars),
            grid=grid,
            in_specs=in_specs,
            out_specs=out_specs,
            scratch_shapes=list(scratch),
        ),
        compiler_params=pltpu.CompilerParams(vmem_limit_bytes=limit),
        cost_estimate=pl.CostEstimate(flops=1 << 10, bytes_accessed=1 << 10, transcendentals=0),
    )(*scalars, *operands)


def whole(shape):
    return pl.BlockSpec(shape, lambda *_: (0,) * len(shape))


def struct(shape, dtype=BF):
    return jax.ShapeDtypeStruct(shape, dtype)


def sigmoid(gates):
    return jax.nn.sigmoid(gates.astype(F32))


def pack_body(in_ref, out_ref):
    for b in range(LOCAL):
        out_ref[:, b] = in_ref[b].reshape(PEERS, ROWS, WIDTH)


def pack(value):
    return call(
        pack_body,
        (),
        (value,),
        [whole((LOCAL, CHANNELS, WIDTH))],
        struct((PEERS, LOCAL, ROWS, WIDTH)),
        whole((PEERS, LOCAL, ROWS, WIDTH)),
    )


def placed(n, core):
    rel = n // SIDE
    real = rel + core - 2 * rel * core
    peer = (n // (LOCAL * ROWS)) % PEERS
    return (peer % 4 * 4 + peer // 4) * (2 * LOCAL) + real * LOCAL + (n // ROWS) % LOCAL


def widen_body(at_ref, sf_ref, wide_ref, turned_ref):
    core = at_ref[0]
    size = 2 * SIDE
    n = lax.broadcasted_iota(jnp.int32, (size, NB), 0)
    o = lax.broadcasted_iota(jnp.int32, (size, NB), 1)
    pick = jnp.where(placed(n, core) == o, 1.0, 0.0).astype(BF)
    row = lax.broadcasted_iota(jnp.int32, (size, size), 0) % ROWS
    column = lax.broadcasted_iota(jnp.int32, (size, size), 1) % ROWS
    same = row == column
    for ref, dim in ((wide_ref, 0), (turned_ref, 1)):
        tall = lax.dot_general(pick, sf_ref[...], (((1,), (dim,)), ((), ())), preferred_element_type=F32)
        full = lax.dot_general(tall.astype(BF), pick, (((1,), (1,)), ((), ())), preferred_element_type=F32)
        ref[...] = jnp.where(same, full, 0.0).astype(BF)


def widen(at, sf):
    shape = (2 * SIDE, 2 * SIDE)
    return call(
        widen_body,
        (at,),
        (sf,),
        [whole((NB, NB))],
        [struct(shape), struct(shape)],
        [whole(shape), whole(shape)],
    )


GROUP = 8
STEP_ROWS = GROUP * LOCAL * ROWS


def forward_body(
    core_ref, in_ref, gate_ref, kernel_ref, ff_ref, mixed_ref, blocks_ref, own_ref, oth_ref, kown_ref, koth_ref, flat
):
    core = core_ref[0]
    for b in range(LOCAL):
        mixed = (in_ref[b].astype(F32) * sigmoid(gate_ref[b])).astype(BF)
        for g in range(GROUP):
            piece = mixed[g * ROWS : (g + 1) * ROWS]
            mixed_ref[g, b] = piece
            flat[(g * LOCAL + b) * ROWS : (g * LOCAL + b + 1) * ROWS] = piece
    blocks = lax.dot_general(flat[...], ff_ref[...], (((1,), (1,)), ((), ())), preferred_element_type=F32)
    blocks = blocks.astype(BF).reshape(GROUP, LOCAL, ROWS, WIDTH)
    blocks_ref[...] = blocks
    for b in range(LOCAL):
        weight = kernel_ref[b].reshape(GROUP, ROWS, WIDTH)
        kern = (blocks[:, b].astype(F32) * weight.astype(F32)).astype(BF)
        low, high = kern[..., :HALF], kern[..., HALF:]
        own_ref[:, b] = jnp.where(core == 0, low, high)
        oth_ref[:, b] = jnp.where(core == 0, high, low)
        low, high = weight[..., :HALF], weight[..., HALF:]
        kown_ref[:, b] = jnp.where(core == 0, low, high)
        koth_ref[:, b] = jnp.where(core == 0, high, low)


def natural_spec():
    return pl.BlockSpec((LOCAL, GROUP * ROWS, WIDTH), lambda i, *_: (0, i, 0))


def rows_spec(width):
    return pl.BlockSpec((GROUP, LOCAL, ROWS, width), lambda i, *_: (i, 0, 0, 0))


def forward(core, inputs, gates, kernel, ff):
    full, part = struct((PEERS, LOCAL, ROWS, WIDTH)), struct((PEERS, LOCAL, ROWS, HALF))
    return call(
        forward_body,
        (core,),
        (inputs, gates, kernel, ff),
        [natural_spec()] * 3 + [whole((WIDTH, WIDTH))],
        [full, full, part, part, part, part],
        [rows_spec(WIDTH)] * 2 + [rows_spec(HALF)] * 4,
        grid=(PEERS // GROUP,),
        scratch=[pltpu.VMEM((STEP_ROWS, WIDTH), BF)],
    )


CHUNK = 256


STEPS = HALF // CHUNK


def across_body(at_ref, wide_ref, own_ref, oth_ref, out_ref):
    own = own_ref[...].reshape(SIDE, CHUNK)
    oth = oth_ref[...].reshape(SIDE, CHUNK)
    total = jnp.dot(wide_ref[:, :SIDE], own, preferred_element_type=F32)
    total = total + jnp.dot(wide_ref[:, SIDE:], oth, preferred_element_type=F32)
    total = total.astype(BF)
    for rel in range(2):
        out_ref[:, rel] = total[rel * SIDE : (rel + 1) * SIDE].reshape(PEERS, LOCAL, ROWS, CHUNK)


def across(at, wide, own, oth, own_spec, oth_spec):
    return call(
        across_body,
        (at,),
        (wide, own, oth),
        [whole((2 * SIDE, 2 * SIDE)), own_spec, oth_spec],
        struct((PEERS, 2, LOCAL, ROWS, HALF)),
        pl.BlockSpec((PEERS, 2, LOCAL, ROWS, CHUNK), lambda i, at: (0, 0, 0, 0, i)),
        grid=(STEPS,),
    )


def across_up(at, wide, up, up_oth):
    block = (PEERS, LOCAL, ROWS, CHUNK)
    own = pl.BlockSpec(block, lambda i, at: (0, 0, 0, at[0] * STEPS + i))
    return across(at, wide, up, up_oth, own, pl.BlockSpec(block, lambda i, at: (0, 0, 0, i)))


def across_kern(at, wide, kern):
    block = (PEERS, 1, LOCAL, ROWS, CHUNK)
    own = pl.BlockSpec(block, lambda i, at: (0, 0, 0, 0, i))
    return across(at, wide, kern, kern, own, pl.BlockSpec(block, lambda i, at: (0, 1, 0, 0, i)))


def second_body(at_ref, up_ref, up_oth_ref, kern_ref, out_ref):
    core = at_ref[0]
    row = lax.broadcasted_iota(jnp.int32, (SIDE, SIDE), 0) % ROWS
    column = lax.broadcasted_iota(jnp.int32, (SIDE, SIDE), 1) % ROWS
    same = row == column
    tall = []
    for ref in (up_ref, up_oth_ref):
        up = ref[...].reshape(SIDE, HALF)
        wide = []
        for rel in range(2):
            kern = kern_ref[:, rel].reshape(SIDE, HALF)
            full = lax.dot_general(up, kern, (((1,), (1,)), ((), ())), preferred_element_type=F32)
            wide.append(jnp.where(same, full, 0.0).reshape(SIDE // ROWS, ROWS, SIDE).sum(1))
        tall.append(jnp.concatenate(wide, 1))
    tall = jnp.concatenate(tall, 0)
    n = lax.broadcasted_iota(jnp.int32, (2 * SIDE, NB), 0)
    o = lax.broadcasted_iota(jnp.int32, (2 * SIDE, NB), 1)
    pick = jnp.where(placed(n, core) == o, 1.0, 0.0)
    total = jnp.dot(tall, pick, precision=lax.Precision.HIGHEST, preferred_element_type=F32)
    n = lax.broadcasted_iota(jnp.int32, (NB, NB), 1) * ROWS
    o = lax.broadcasted_iota(jnp.int32, (NB, NB), 0)
    pick = jnp.where(placed(n, core) == o, 1.0, 0.0)
    out_ref[...] = jnp.dot(pick, total, precision=lax.Precision.HIGHEST, preferred_element_type=F32)


def second(at, up, up_oth, kern):
    block = (PEERS, LOCAL, ROWS, HALF)
    return call(
        second_body,
        (at,),
        (up, up_oth, kern),
        [pl.BlockSpec(block, lambda i, at: (0, 0, 0, at[0])), whole(block), whole(kern.shape)],
        struct((NB, NB), F32),
        whole((NB, NB)),
    )


SHARE = HALF // 4
PACKED = WIDTH + NB


def first_body(x_ref, at_ref, mid_ref, kown_ref, koth_ref, own_ref, oth_ref, second_ref, *refs):
    total = 0.0
    for rel, (weight, mixed) in enumerate(((kown_ref, own_ref), (koth_ref, oth_ref))):
        grad = mid_ref[:, rel].reshape(SIDE, HALF) * weight[...].reshape(SIDE, HALF)
        total = total + lax.dot_general(
            grad, mixed[...].reshape(SIDE, WIDTH), (((0,), (0,)), ((), ())), preferred_element_type=F32
        )
    full_ref = refs[4]
    full_ref[...] = total
    row = lax.broadcasted_iota(jnp.int32, (SHARE, NB), 0)
    column = lax.broadcasted_iota(jnp.int32, (SHARE, NB), 1)
    for step, ref in zip((2, 1, 3, 0), refs):
        x = lax.rem(x_ref[0] + step, 4)
        high, low = x // 2, lax.rem(x, 2)
        for y in range(4):
            rows = pl.ds(pl.multiple_of((high * 8 + 2 * y + low) * 32, 32), 32)
            ref[y * 32 : (y + 1) * 32, :WIDTH] = full_ref[rows, :].astype(ref.dtype)
        place = (2 * at_ref[0] + high) * 8 + row // 32 * 2 + low
        pick = jnp.where((place * LOCAL + row % 32 == column) & (row % 32 < LOCAL), 1.0, 0.0)
        terms = jnp.dot(pick, second_ref[...], precision=lax.Precision.HIGHEST, preferred_element_type=F32)
        ref[:, WIDTH:] = terms.astype(ref.dtype)


def first_terms(x, at, mid, kown, koth, own, oth, terms):
    out = (SHARE, PACKED)
    operands = (mid, kown, koth, own, oth, terms)
    return call(
        first_body,
        (x, at),
        operands,
        [whole(operand.shape) for operand in operands],
        [struct(out), struct(out), struct(out), struct(out, F32)],
        [whole(out)] * 4,
        limit=40 * 1024 * 1024,
        scratch=[pltpu.VMEM((HALF, WIDTH), F32)],
    )


def grads_body(
    core_ref, mid_ref, got_ref, blocks_ref, kown_ref, koth_ref, in_ref, gate_ref, ff_ref, gin_ref, ggate_ref, gkern_ref
):
    core = core_ref[0]
    own = pl.ds(pl.multiple_of(core * HALF, HALF), HALF)
    oth = pl.ds(pl.multiple_of((1 - core) * HALF, HALF), HALF)
    total = 0.0
    for at, mid, weight in ((own, mid_ref[:, 0], kown_ref), (oth, got_ref[...], koth_ref)):
        grad = mid * blocks_ref[:, :, :, at]
        for b in range(LOCAL):
            gkern_ref[b, :, at] = grad[:, b].reshape(GROUP * ROWS, HALF)
        grad = (mid * weight[...]).reshape(STEP_ROWS, HALF)
        total = total + jnp.dot(grad, ff_ref[at, :], preferred_element_type=F32)
    total = total.reshape(GROUP, LOCAL, ROWS, WIDTH)
    for b in range(LOCAL):
        grad = total[:, b].reshape(GROUP * ROWS, WIDTH)
        sig = sigmoid(gate_ref[b])
        gin_ref[b] = (grad * sig).astype(BF)
        ggate_ref[b] = (grad * in_ref[b].astype(F32) * sig * (1.0 - sig)).astype(BF)


def grads(core, mid, got, blocks, kown, koth, inputs, gates, ff):
    out = struct((LOCAL, CHANNELS, WIDTH))
    return call(
        grads_body,
        (core,),
        (mid, got, blocks, kown, koth, inputs, gates, ff),
        [
            pl.BlockSpec((GROUP, 1, LOCAL, ROWS, HALF), lambda i, *_: (i, 0, 0, 0, 0)),
            rows_spec(HALF),
            rows_spec(WIDTH),
            rows_spec(HALF),
            rows_spec(HALF),
            natural_spec(),
            natural_spec(),
            whole((WIDTH, WIDTH)),
        ],
        [out, out, out],
        [natural_spec()] * 3,
        grid=(PEERS // GROUP,),
    )


def join_body(core_ref, mid_ref, got_ref, out_ref):
    core = core_ref[0]
    own = pl.ds(pl.multiple_of(core * HALF, HALF), HALF)
    oth = pl.ds(pl.multiple_of((1 - core) * HALF, HALF), HALF)
    for b in range(LOCAL):
        out_ref[b, :, own] = mid_ref[:, 0, b].reshape(GROUP * ROWS, HALF)
        out_ref[b, :, oth] = got_ref[:, b].reshape(GROUP * ROWS, HALF)


def join(core, mid, got):
    return call(
        join_body,
        (core,),
        (mid, got),
        [pl.BlockSpec((GROUP, 1, LOCAL, ROWS, HALF), lambda i, *_: (i, 0, 0, 0, 0)), rows_spec(HALF)],
        struct((LOCAL, CHANNELS, WIDTH)),
        natural_spec(),
        grid=(PEERS // GROUP,),
    )


def on_device(inputs, gates, kernel, first_factor, second_factor, upstream):
    core, x, y = (lax.axis_index(axis).astype(jnp.int32) for axis in ("c", "x", "y"))
    x_at, at = x.reshape(1), core.reshape(1)
    all_channels = CHANNELS * lax.axis_size("zl") * lax.axis_size("x")

    up = exchange(pack(upstream))
    mixed, blocks, kern_own, kern_oth, kown, koth = forward(at, inputs, gates, kernel, first_factor)
    kern = jnp.stack([kern_own, swap(kern_oth)], 1)
    wide, turned = widen(at, second_factor)
    up, kern, wide, turned = lax.optimization_barrier((up, kern, wide, turned))

    kern = exchange(kern)
    up_oth = swap(lax.dynamic_slice_in_dim(up, (1 - core) * HALF, HALF, 3))
    mid = across_up(at, turned, up, up_oth)
    koth_got = swap(koth)
    mixed_got = swap(mixed)
    mid, kern, koth_got, mixed_got = lax.optimization_barrier((mid, kern, koth_got, mixed_got))

    mid = exchange(mid)
    out = across_kern(at, wide, kern)

    terms = second(at, up, up_oth, kern)
    terms = terms + swap(terms)
    mid, out, terms = lax.optimization_barrier((mid, out, terms))
    out = exchange(out)

    sent2, sent1, sent3, total = first_terms(x_at, at, mid, kown, koth_got, mixed, mixed_got, terms)
    got = [shift(sent2, "x", 2), shift(sent1, "x", 1), shift(sent3, "x", 3)]
    mid_got = swap(mid[:, 1])
    others = grads(at, mid, mid_got, blocks, kown, koth, inputs, gates, first_factor)
    total, *others = lax.optimization_barrier((total, *others))

    total = total + got[1].astype(F32) + got[2].astype(F32) + got[0].astype(F32)
    total = total.reshape(4, SHARE // 4, PACKED)
    parts = total.astype(BF)
    got = [shift(lax.dynamic_index_in_dim(parts, lax.rem(y + step, 4), 0, False), "y", step) for step in (2, 1, 3)]
    total = lax.dynamic_index_in_dim(total, y, 0, False)
    for part in got:
        total = total + part.astype(F32)
    part = total.astype(BF)
    near = flip(part, "zl", 1)
    output = join(at, out, swap(out[:, 1]))
    part, output = lax.optimization_barrier((part, output))
    part = (part.astype(F32) + near.astype(F32)).astype(BF)
    got = [lax.ppermute(part, AXES, to_owner(step)).astype(F32) for step in range(4)]
    total = (got[0] + got[1]) + (got[2] + got[3])
    grad_first = total[:, :WIDTH] * (1.0 / math.sqrt(NB * all_channels))
    grad_second = total[:LOCAL, WIDTH:] * (1.0 / math.sqrt(all_channels * WIDTH))
    return (output, *others, grad_first, grad_second)


def solution(mesh):
    fine = Mesh(mesh.devices.reshape(2, 4, 4, 4, 2), AXES)
    seq, dp = ("zh", "y", "c"), ("zl", "x")
    big = P(seq, dp, None)
    return jax.shard_map(
        on_device,
        mesh=fine,
        in_specs=(big, big, big, P(), P(), big),
        out_specs=(big, big, big, big, P(seq, None), P(seq, None)),
        check_vma=False,
    )
```

```python
import math

import jax
import jax.numpy as jnp
from jax import lax
from jax.experimental import pallas as pl
from jax.experimental.pallas import tpu as pltpu
from jax.sharding import Mesh
from jax.sharding import PartitionSpec as P

AXES = ("zl", "x", "zh", "y", "c")
BF = jnp.bfloat16
F32 = jnp.float32
PEERS, LOCAL, ROWS, HALF = 16, 4, 8, 512
CHANNELS, WIDTH = PEERS * ROWS, 2 * HALF
NB = PEERS * 2 * LOCAL
SIDE = PEERS * LOCAL * ROWS
LIMIT = 60 * 1024 * 1024


def swap(value):
    return lax.ppermute(value, "c", [(0, 1), (1, 0)])


def flip(value, axis, bit):
    size = lax.axis_size(axis)
    return lax.ppermute(value, axis, [(i, i ^ bit) for i in range(size)])


def shift(value, axis, step):
    size = lax.axis_size(axis)
    return lax.ppermute(value, axis, [(i, (i + step) % size) for i in range(size)])


def exchange(value):
    return lax.all_to_all(value, ("y", "zh"), 0, 0, tiled=True)


def to_owner(step):
    perm = []
    for zl in range(2):
        for x in range(4):
            for zh in range(4):
                for y in range(4):
                    for c in range(2):
                        place = (2 * c + x // 2) * 8 + 2 * y + x % 2
                        source = (((zl * 4 + x) * 4 + zh) * 4 + y) * 2 + c
                        target = (((zl * 4 + (zh ^ step)) * 4 + place // 8) * 4 + place // 2 % 4) * 2 + place % 2
                        perm.append((source, target))
    return perm


def call(body, scalars, operands, in_specs, out_shapes, out_specs, grid=(1,), scratch=(), limit=LIMIT):
    return pl.pallas_call(
        body,
        out_shape=out_shapes,
        grid_spec=pltpu.PrefetchScalarGridSpec(
            num_scalar_prefetch=len(scalars),
            grid=grid,
            in_specs=in_specs,
            out_specs=out_specs,
            scratch_shapes=list(scratch),
        ),
        compiler_params=pltpu.CompilerParams(vmem_limit_bytes=limit),
        cost_estimate=pl.CostEstimate(flops=1 << 10, bytes_accessed=1 << 10, transcendentals=0),
    )(*scalars, *operands)


def whole(shape):
    return pl.BlockSpec(shape, lambda *_: (0,) * len(shape))


def struct(shape, dtype=BF):
    return jax.ShapeDtypeStruct(shape, dtype)


def sigmoid(gates):
    return jax.nn.sigmoid(gates.astype(F32))


def pack_body(in_ref, out_ref):
    for b in range(LOCAL):
        out_ref[:, b] = in_ref[b].reshape(PEERS, ROWS, WIDTH)


def pack(value):
    return call(
        pack_body,
        (),
        (value,),
        [whole((LOCAL, CHANNELS, WIDTH))],
        struct((PEERS, LOCAL, ROWS, WIDTH)),
        whole((PEERS, LOCAL, ROWS, WIDTH)),
        limit=16 * 1024 * 1024,
    )


def placed(n, core):
    rel = n // SIDE
    real = rel + core - 2 * rel * core
    peer = (n // (LOCAL * ROWS)) % PEERS
    return (peer % 4 * 4 + peer // 4) * (2 * LOCAL) + real * LOCAL + (n // ROWS) % LOCAL


def widen_body(at_ref, sf_ref, wide_ref, turned_ref):
    core = at_ref[0]
    size = 2 * SIDE
    n = lax.broadcasted_iota(jnp.int32, (size, NB), 0)
    o = lax.broadcasted_iota(jnp.int32, (size, NB), 1)
    pick = jnp.where(placed(n, core) == o, 1.0, 0.0).astype(BF)
    row = lax.broadcasted_iota(jnp.int32, (size, size), 0) % ROWS
    column = lax.broadcasted_iota(jnp.int32, (size, size), 1) % ROWS
    same = row == column
    for ref, dim in ((wide_ref, 0), (turned_ref, 1)):
        tall = lax.dot_general(pick, sf_ref[...], (((1,), (dim,)), ((), ())), preferred_element_type=F32)
        full = lax.dot_general(tall.astype(BF), pick, (((1,), (1,)), ((), ())), preferred_element_type=F32)
        ref[...] = jnp.where(same, full, 0.0).astype(BF)


def widen(at, sf):
    shape = (2 * SIDE, 2 * SIDE)
    return call(
        widen_body,
        (at,),
        (sf,),
        [whole((NB, NB))],
        [struct(shape), struct(shape)],
        [whole(shape), whole(shape)],
    )


GROUP = 8
STEP_ROWS = GROUP * LOCAL * ROWS


def forward_body(
    core_ref, in_ref, gate_ref, kernel_ref, ff_ref, mixed_ref, blocks_ref, own_ref, oth_ref, kown_ref, koth_ref, flat
):
    core = core_ref[0]
    for b in range(LOCAL):
        mixed = (in_ref[b].astype(F32) * sigmoid(gate_ref[b])).astype(BF)
        for g in range(GROUP):
            piece = mixed[g * ROWS : (g + 1) * ROWS]
            mixed_ref[g, b] = piece
            flat[(g * LOCAL + b) * ROWS : (g * LOCAL + b + 1) * ROWS] = piece
    blocks = lax.dot_general(flat[...], ff_ref[...], (((1,), (1,)), ((), ())), preferred_element_type=F32)
    blocks = blocks.astype(BF).reshape(GROUP, LOCAL, ROWS, WIDTH)
    blocks_ref[...] = blocks
    for b in range(LOCAL):
        weight = kernel_ref[b].reshape(GROUP, ROWS, WIDTH)
        kern = (blocks[:, b].astype(F32) * weight.astype(F32)).astype(BF)
        low, high = kern[..., :HALF], kern[..., HALF:]
        own_ref[:, b] = jnp.where(core == 0, low, high)
        oth_ref[:, b] = jnp.where(core == 0, high, low)
        low, high = weight[..., :HALF], weight[..., HALF:]
        kown_ref[:, b] = jnp.where(core == 0, low, high)
        koth_ref[:, b] = jnp.where(core == 0, high, low)


def natural_spec():
    return pl.BlockSpec((LOCAL, GROUP * ROWS, WIDTH), lambda i, *_: (0, i, 0))


def rows_spec(width):
    return pl.BlockSpec((GROUP, LOCAL, ROWS, width), lambda i, *_: (i, 0, 0, 0))


def forward(core, inputs, gates, kernel, ff):
    full, part = struct((PEERS, LOCAL, ROWS, WIDTH)), struct((PEERS, LOCAL, ROWS, HALF))
    return call(
        forward_body,
        (core,),
        (inputs, gates, kernel, ff),
        [natural_spec()] * 3 + [whole((WIDTH, WIDTH))],
        [full, full, part, part, part, part],
        [rows_spec(WIDTH)] * 2 + [rows_spec(HALF)] * 4,
        grid=(PEERS // GROUP,),
        scratch=[pltpu.VMEM((STEP_ROWS, WIDTH), BF)],
    )


CHUNK = 256


STEPS = HALF // CHUNK


def across_body(at_ref, wide_ref, own_ref, oth_ref, out_ref):
    own = own_ref[...].reshape(SIDE, CHUNK)
    oth = oth_ref[...].reshape(SIDE, CHUNK)
    total = jnp.dot(wide_ref[:, :SIDE], own, preferred_element_type=F32)
    total = total + jnp.dot(wide_ref[:, SIDE:], oth, preferred_element_type=F32)
    total = total.astype(BF)
    for rel in range(2):
        out_ref[:, rel] = total[rel * SIDE : (rel + 1) * SIDE].reshape(PEERS, LOCAL, ROWS, CHUNK)


def across(at, wide, own, oth, own_spec, oth_spec):
    return call(
        across_body,
        (at,),
        (wide, own, oth),
        [whole((2 * SIDE, 2 * SIDE)), own_spec, oth_spec],
        struct((PEERS, 2, LOCAL, ROWS, HALF)),
        pl.BlockSpec((PEERS, 2, LOCAL, ROWS, CHUNK), lambda i, at: (0, 0, 0, 0, i)),
        grid=(STEPS,),
    )


def across_up(at, wide, up, up_oth):
    block = (PEERS, LOCAL, ROWS, CHUNK)
    own = pl.BlockSpec(block, lambda i, at: (0, 0, 0, at[0] * STEPS + i))
    return across(at, wide, up, up_oth, own, pl.BlockSpec(block, lambda i, at: (0, 0, 0, i)))


def across_kern(at, wide, kern):
    block = (PEERS, 1, LOCAL, ROWS, CHUNK)
    own = pl.BlockSpec(block, lambda i, at: (0, 0, 0, 0, i))
    return across(at, wide, kern, kern, own, pl.BlockSpec(block, lambda i, at: (0, 1, 0, 0, i)))


def second_body(at_ref, up_ref, up_oth_ref, kern_ref, out_ref):
    core = at_ref[0]
    row = lax.broadcasted_iota(jnp.int32, (SIDE, SIDE), 0) % ROWS
    column = lax.broadcasted_iota(jnp.int32, (SIDE, SIDE), 1) % ROWS
    same = row == column
    tall = []
    for ref in (up_ref, up_oth_ref):
        up = ref[...].reshape(SIDE, HALF)
        wide = []
        for rel in range(2):
            kern = kern_ref[:, rel].reshape(SIDE, HALF)
            full = lax.dot_general(up, kern, (((1,), (1,)), ((), ())), preferred_element_type=F32)
            wide.append(jnp.where(same, full, 0.0).reshape(SIDE // ROWS, ROWS, SIDE).sum(1))
        tall.append(jnp.concatenate(wide, 1))
    tall = jnp.concatenate(tall, 0)
    n = lax.broadcasted_iota(jnp.int32, (2 * SIDE, NB), 0)
    o = lax.broadcasted_iota(jnp.int32, (2 * SIDE, NB), 1)
    pick = jnp.where(placed(n, core) == o, 1.0, 0.0)
    total = jnp.dot(tall, pick, precision=lax.Precision.HIGHEST, preferred_element_type=F32)
    n = lax.broadcasted_iota(jnp.int32, (NB, NB), 1) * ROWS
    o = lax.broadcasted_iota(jnp.int32, (NB, NB), 0)
    pick = jnp.where(placed(n, core) == o, 1.0, 0.0)
    out_ref[...] = jnp.dot(pick, total, precision=lax.Precision.HIGHEST, preferred_element_type=F32)


def second(at, up, up_oth, kern):
    block = (PEERS, LOCAL, ROWS, HALF)
    return call(
        second_body,
        (at,),
        (up, up_oth, kern),
        [pl.BlockSpec(block, lambda i, at: (0, 0, 0, at[0])), whole(block), whole(kern.shape)],
        struct((NB, NB), F32),
        whole((NB, NB)),
    )


SHARE = HALF // 4
PACKED = WIDTH + NB


def first_body(x_ref, at_ref, mid_ref, kown_ref, koth_ref, own_ref, oth_ref, second_ref, *refs):
    total = 0.0
    for rel, (weight, mixed) in enumerate(((kown_ref, own_ref), (koth_ref, oth_ref))):
        grad = mid_ref[:, rel].reshape(SIDE, HALF) * weight[...].reshape(SIDE, HALF)
        total = total + lax.dot_general(
            grad, mixed[...].reshape(SIDE, WIDTH), (((0,), (0,)), ((), ())), preferred_element_type=F32
        )
    full_ref = refs[4]
    full_ref[...] = total
    row = lax.broadcasted_iota(jnp.int32, (SHARE, NB), 0)
    column = lax.broadcasted_iota(jnp.int32, (SHARE, NB), 1)
    for step, ref in zip((2, 1, 3, 0), refs):
        x = lax.rem(x_ref[0] + step, 4)
        high, low = x // 2, lax.rem(x, 2)
        for y in range(4):
            rows = pl.ds(pl.multiple_of((high * 8 + 2 * y + low) * 32, 32), 32)
            ref[y * 32 : (y + 1) * 32, :WIDTH] = full_ref[rows, :].astype(ref.dtype)
        place = (2 * at_ref[0] + high) * 8 + row // 32 * 2 + low
        pick = jnp.where((place * LOCAL + row % 32 == column) & (row % 32 < LOCAL), 1.0, 0.0)
        terms = jnp.dot(pick, second_ref[...], precision=lax.Precision.HIGHEST, preferred_element_type=F32)
        ref[:, WIDTH:] = terms.astype(ref.dtype)


def first_terms(x, at, mid, kown, koth, own, oth, terms):
    out = (SHARE, PACKED)
    operands = (mid, kown, koth, own, oth, terms)
    return call(
        first_body,
        (x, at),
        operands,
        [whole(operand.shape) for operand in operands],
        [struct(out), struct(out), struct(out), struct(out, F32)],
        [whole(out)] * 4,
        limit=40 * 1024 * 1024,
        scratch=[pltpu.VMEM((HALF, WIDTH), F32)],
    )


def grads_body(
    core_ref, mid_ref, got_ref, blocks_ref, kown_ref, koth_ref, in_ref, gate_ref, ff_ref, gin_ref, ggate_ref, gkern_ref
):
    core = core_ref[0]
    own = pl.ds(pl.multiple_of(core * HALF, HALF), HALF)
    oth = pl.ds(pl.multiple_of((1 - core) * HALF, HALF), HALF)
    total = 0.0
    for at, mid, weight in ((own, mid_ref[:, 0], kown_ref), (oth, got_ref[...], koth_ref)):
        grad = mid * blocks_ref[:, :, :, at]
        for b in range(LOCAL):
            gkern_ref[b, :, at] = grad[:, b].reshape(GROUP * ROWS, HALF)
        grad = (mid * weight[...]).reshape(STEP_ROWS, HALF)
        total = total + jnp.dot(grad, ff_ref[at, :], preferred_element_type=F32)
    total = total.reshape(GROUP, LOCAL, ROWS, WIDTH)
    for b in range(LOCAL):
        grad = total[:, b].reshape(GROUP * ROWS, WIDTH)
        sig = sigmoid(gate_ref[b])
        gin_ref[b] = (grad * sig).astype(BF)
        ggate_ref[b] = (grad * in_ref[b].astype(F32) * sig * (1.0 - sig)).astype(BF)


def grads(core, mid, got, blocks, kown, koth, inputs, gates, ff):
    out = struct((LOCAL, CHANNELS, WIDTH))
    return call(
        grads_body,
        (core,),
        (mid, got, blocks, kown, koth, inputs, gates, ff),
        [
            pl.BlockSpec((GROUP, 1, LOCAL, ROWS, HALF), lambda i, *_: (i, 0, 0, 0, 0)),
            rows_spec(HALF),
            rows_spec(WIDTH),
            rows_spec(HALF),
            rows_spec(HALF),
            natural_spec(),
            natural_spec(),
            whole((WIDTH, WIDTH)),
        ],
        [out, out, out],
        [natural_spec()] * 3,
        grid=(PEERS // GROUP,),
    )


def join_body(core_ref, mid_ref, got_ref, out_ref):
    core = core_ref[0]
    own = pl.ds(pl.multiple_of(core * HALF, HALF), HALF)
    oth = pl.ds(pl.multiple_of((1 - core) * HALF, HALF), HALF)
    for b in range(LOCAL):
        out_ref[b, :, own] = mid_ref[:, 0, b].reshape(GROUP * ROWS, HALF)
        out_ref[b, :, oth] = got_ref[:, b].reshape(GROUP * ROWS, HALF)


def join(core, mid, got):
    return call(
        join_body,
        (core,),
        (mid, got),
        [pl.BlockSpec((GROUP, 1, LOCAL, ROWS, HALF), lambda i, *_: (i, 0, 0, 0, 0)), rows_spec(HALF)],
        struct((LOCAL, CHANNELS, WIDTH)),
        natural_spec(),
        grid=(PEERS // GROUP,),
    )


def on_device(inputs, gates, kernel, first_factor, second_factor, upstream):
    core, x, y = (lax.axis_index(axis).astype(jnp.int32) for axis in ("c", "x", "y"))
    x_at, at = x.reshape(1), core.reshape(1)
    all_channels = CHANNELS * lax.axis_size("zl") * lax.axis_size("x")

    up = exchange(pack(upstream))
    mixed, blocks, kern_own, kern_oth, kown, koth = forward(at, inputs, gates, kernel, first_factor)
    kern = jnp.stack([kern_own, swap(kern_oth)], 1)
    wide, turned = widen(at, second_factor)
    up, kern, wide, turned = lax.optimization_barrier((up, kern, wide, turned))

    kern = exchange(kern)
    up_oth = swap(lax.dynamic_slice_in_dim(up, (1 - core) * HALF, HALF, 3))
    mid = across_up(at, turned, up, up_oth)
    koth_got = swap(koth)
    mixed_got = swap(mixed)
    mid, kern, koth_got, mixed_got = lax.optimization_barrier((mid, kern, koth_got, mixed_got))

    mid = exchange(mid)
    out = across_kern(at, wide, kern)

    terms = second(at, up, up_oth, kern)
    terms = terms + swap(terms)
    mid, out, terms = lax.optimization_barrier((mid, out, terms))
    out = exchange(out)

    sent2, sent1, sent3, total = first_terms(x_at, at, mid, kown, koth_got, mixed, mixed_got, terms)
    got = [shift(sent2, "x", 2), shift(sent1, "x", 1), shift(sent3, "x", 3)]
    mid_got = swap(mid[:, 1])
    others = grads(at, mid, mid_got, blocks, kown, koth, inputs, gates, first_factor)
    total, *others = lax.optimization_barrier((total, *others))

    total = total + got[1].astype(F32) + got[2].astype(F32) + got[0].astype(F32)
    total = total.reshape(4, SHARE // 4, PACKED)
    parts = total.astype(BF)
    got = [shift(lax.dynamic_index_in_dim(parts, lax.rem(y + step, 4), 0, False), "y", step) for step in (2, 1, 3)]
    total = lax.dynamic_index_in_dim(total, y, 0, False)
    for part in got:
        total = total + part.astype(F32)
    part = total.astype(BF)
    near = flip(part, "zl", 1)
    output = join(at, out, swap(out[:, 1]))
    part, output = lax.optimization_barrier((part, output))
    part = (part.astype(F32) + near.astype(F32)).astype(BF)
    got = [lax.ppermute(part, AXES, to_owner(step)).astype(F32) for step in range(4)]
    total = (got[0] + got[1]) + (got[2] + got[3])
    grad_first = total[:, :WIDTH] * (1.0 / math.sqrt(NB * all_channels))
    grad_second = total[:LOCAL, WIDTH:] * (1.0 / math.sqrt(all_channels * WIDTH))
    return (output, *others, grad_first, grad_second)


def solution(mesh):
    fine = Mesh(mesh.devices.reshape(2, 4, 4, 4, 2), AXES)
    seq, dp = ("zh", "y", "c"), ("zl", "x")
    big = P(seq, dp, None)
    return jax.shard_map(
        on_device,
        mesh=fine,
        in_specs=(big, big, big, P(), P(), big),
        out_specs=(big, big, big, big, P(seq, None), P(seq, None)),
        check_vma=False,
    )
```
